512 devices in a mesh: row: 16 (over z_hi, y), col: 8 (over z_lo, core), seq: 4 (over x).
Axes of the slice: x: 4, y: 8, z: 8 (z_hi: 2, z_lo: 4; z = z_hi * 4 + z_lo), core: 2. Of those that a mesh axis runs over, the one named last changes fastest.
Arguments:
- alignment_embedding: bfloat16 [128, 1024, 256], P('seq', ('row', 'col')), may hold values from -8 to 8
- standardize_scale: float32 [256], replicated, may hold values from 0.5 to 1.5
- standardize_shift: float32 [256], replicated, may hold values from -3 to 3
- left_mapping_matrix: bfloat16 [256, 32], replicated, may hold values from -0.375 to 0.375
- left_offset_term: float32 [32], replicated, may hold values from -3 to 3
- right_mapping_matrix: bfloat16 [256, 32], replicated, may hold values from -0.375 to 0.375
- right_offset_term: float32 [32], replicated, may hold values from -3 to 3
- final_mapping_matrix: float32 [1024, 128], replicated, may hold values from -0.1875 to 0.1875
- final_offset_term: float32 [128], replicated, may hold values from -4 to 4
Outputs:
- paired: bfloat16 [1024, 1024, 128], P(('row', 'seq'), 'col')
The draws below stay inside these ranges and needn't reach their ends.
All inputs are finite; a program needn't handle non-finite values.
Results may differ from the reference program's by a relative error of at most 0.013.
Values may be sent and summed in bfloat16 or wider, within the bound.
No kernel may reach another device: no remote copies, remote signals or barrier semaphores. Data moves between devices by JAX's collectives and lax.ppermute only.
A program may use at most 64 MiB of HBM per device.

```python
import jax
import jax.numpy as jnp
from jax import lax

CM = 256
CA = 32
CZ = 128
R = 1024
S = 128


def draw_alignment_embedding(key, part):
    key = jax.random.fold_in(key, 17)
    prof_key, noise_key = jax.random.split(key, 2)
    profile = jax.random.normal(prof_key, (R, CM), jnp.float32)
    noise = jax.random.normal(noise_key, (S, R, CM), jnp.float32)
    return jnp.clip(profile[None] + noise, -8.0, 8.0).astype(jnp.bfloat16)


def bell_draw(key, extent, scale, limit, kind=jnp.bfloat16):
    return jnp.clip(scale * jax.random.normal(key, extent, jnp.float32), -limit, limit).astype(kind)


def setup_inputs(seed: int = 0) -> dict:
    splits = jax.random.split(jax.random.key(seed), 10)
    return {
        "alignment_embedding": draw_alignment_embedding(jax.random.fold_in(splits[9], 71), 0),
        "standardize_scale": jnp.clip(jax.random.uniform(splits[1], (CM,), jnp.float32, 0.5, 1.5), 0.5, 1.5),
        "standardize_shift": bell_draw(splits[2], (CM,), 0.5, 3.0, jnp.float32),
        "left_mapping_matrix": bell_draw(splits[3], (CM, CA), CM ** -0.5, 0.375),
        "left_offset_term": bell_draw(splits[4], (CA,), 0.5, 3.0, jnp.float32),
        "right_mapping_matrix": bell_draw(splits[5], (CM, CA), CM ** -0.5, 0.375),
        "right_offset_term": bell_draw(splits[6], (CA,), 0.5, 3.0, jnp.float32),
        "final_mapping_matrix": bell_draw(splits[7], (CA * CA, CZ), (CA * CA) ** -0.5, 0.1875, jnp.float32),
        "final_offset_term": bell_draw(splits[8], (CZ,), 1.0, 4.0, jnp.float32),
    }


def standardize_features(alignment_embedding, standardize_scale, standardize_shift):
    incoming_tensor = alignment_embedding.astype(jnp.float32)
    avg_chan = lax.optimization_barrier(jnp.mean(incoming_tensor, axis=-1, keepdims=True))
    centered = incoming_tensor - avg_chan
    spread_sq = lax.optimization_barrier(jnp.mean(centered * centered, axis=-1, keepdims=True))
    return (centered * lax.rsqrt(spread_sq + 1e-05) * standardize_scale + standardize_shift).astype(jnp.bfloat16)

def project_in(standardized_tensor, weight, bias):
    flat_rows = standardized_tensor.reshape(-1, standardized_tensor.shape[-1])
    result = jnp.dot(flat_rows, weight, preferred_element_type=jnp.float32) + bias
    return result.astype(jnp.bfloat16).reshape(standardized_tensor.shape[0], standardized_tensor.shape[1], weight.shape[1])

def reference(alignment_embedding, standardize_scale, standardize_shift, left_mapping_matrix, left_offset_term, right_mapping_matrix, right_offset_term, final_mapping_matrix, final_offset_term):
    standardized_tensor = standardize_features(alignment_embedding, standardize_scale, standardize_shift)
    left_proj = project_in(standardized_tensor, left_mapping_matrix, left_offset_term).astype(jnp.float32)
    right_proj = project_in(standardized_tensor, right_mapping_matrix, right_offset_term).astype(jnp.float32)
    block_rows = 8
    inv_count = jnp.float32(1.0 / S)
    row_blocks = left_proj.reshape(S, R // block_rows, block_rows, CA).transpose(1, 0, 2, 3)

    def one_block(block):
        outer_sum = jnp.einsum('sic,sje->ijce', block, right_proj, precision=lax.Precision.HIGHEST)
        flat_outer = outer_sum.reshape(block_rows * R, CA * CA) * inv_count
        result = jnp.dot(flat_outer, final_mapping_matrix, precision=lax.Precision.HIGHEST) + final_offset_term
        return result.astype(jnp.bfloat16).reshape(block_rows, R, CZ)
    return lax.map(one_block, row_blocks).reshape(R, R, CZ)
```

```python
import jax
import jax.numpy as jnp
from jax import lax
from jax.experimental import pallas as pl
from jax.experimental.pallas import tpu as pltpu
from jax.sharding import PartitionSpec as P

MESH_AXES = ("row", "col", "seq")
BF16, F32 = jnp.bfloat16, jnp.float32


def project_kernel(x_ref, scale_ref, shift_ref, wl_ref, bl_ref, wr_ref, br_ref, left_ref, right_ref):
    rows, width = x_ref.shape
    proj = wl_ref.shape[1]
    deep, wide = left_ref.shape[-2:]
    resid = rows // deep
    x = x_ref[...].astype(F32)
    mean = jnp.sum(x, axis=-1, keepdims=True) * (1.0 / width)
    centered = x - mean
    spread = jnp.sum(centered * centered, axis=-1, keepdims=True) * (1.0 / width)
    normed = (centered * lax.rsqrt(spread + 1e-5) * scale_ref[...] + shift_ref[...]).astype(BF16)
    weight = jnp.concatenate([wl_ref[...], wr_ref[...]], axis=1)
    bias = jnp.concatenate([bl_ref[...], br_ref[...]], axis=1)
    both = (jnp.dot(normed, weight, preferred_element_type=F32) + bias).astype(BF16)
    chan = lax.broadcasted_iota(jnp.int32, (2 * proj, 2 * wide), 0)
    lane = lax.broadcasted_iota(jnp.int32, (2 * proj, 2 * wide), 1)
    wanted = jnp.where(lane < wide, lane % proj, proj + (lane - wide) // resid)
    expand = jnp.where(chan == wanted, 1.0, 0.0).astype(BF16)
    spread_out = jnp.dot(both, expand, preferred_element_type=F32)
    lane = lax.broadcasted_iota(jnp.int32, (resid, 2 * wide), 1)
    own = lax.broadcasted_iota(jnp.int32, (resid, 2 * wide), 0)
    keep = jnp.where(own == jnp.where(lane < wide, lane // proj, lane % resid), 1.0, 0.0)
    kept = (spread_out.reshape(deep, resid, 2 * wide) * keep[None]).reshape(rows, 2 * wide).astype(BF16)
    seq = lax.broadcasted_iota(jnp.int32, (deep, rows), 0)
    tok = lax.broadcasted_iota(jnp.int32, (deep, rows), 1)
    fold = jnp.where(tok // resid == seq, 1.0, 0.0).astype(BF16)
    packed = jnp.dot(fold, kept, preferred_element_type=F32).astype(BF16)
    left_ref[...] = jnp.broadcast_to(packed[:, :wide], left_ref.shape)
    right_ref[...] = jnp.broadcast_to(packed[:, wide:], right_ref.shape)


def project(x, scale, shift, wl, bl, wr, br, left_copies, right_copies):
    deep, resid, width = x.shape
    proj = wl.shape[1]
    return pl.pallas_call(
        project_kernel,
        out_shape=[
            jax.ShapeDtypeStruct((*left_copies, deep, resid * proj), BF16),
            jax.ShapeDtypeStruct((*right_copies, deep, resid * proj), BF16),
        ],
        compiler_params=pltpu.CompilerParams(vmem_limit_bytes=32 * 1024 * 1024),
        name="project",
    )(
        x.reshape(deep * resid, width),
        scale.reshape(1, -1),
        shift.reshape(1, -1),
        wl,
        bl.reshape(1, -1),
        wr,
        br.reshape(1, -1),
    )


def pair_kernel(get_left, get_right, sizes, *refs):
    (*in_refs, w_ref, b_ref, out_ref, lt, rt, outer) = refs
    n_seq, deep, resid, proj, jblocks, iblocks = sizes
    S = n_seq * deep
    lanes = 128
    per_l = lanes // proj
    per_r = lanes // resid
    halves = resid * proj // lanes
    for ib in range(iblocks):
        for h in range(halves):
            t = get_left(in_refs, ib, h).astype(F32).T
            lt[pl.ds((ib * halves + h) * lanes, lanes), :] = t.astype(BF16)

    def turn(jb, _):
        for h in range(halves):
            t = get_right(in_refs, jb, h).astype(F32).T
            rt[pl.ds(h * per_r, per_r), pl.ds(pl.multiple_of(jb * resid, resid), resid), :] = t.reshape(per_r, resid, S)
        return 0

    lax.fori_loop(0, jblocks, turn, 0)
    left = lt[...]
    n_i = iblocks * resid
    cols = jblocks * resid

    def one_pair(p, _):
        r = rt[pl.ds(p * 2, 2)].reshape(2 * cols, S).astype(BF16)
        o = lax.dot_general(left, r, (((1,), (1,)), ((), ())), preferred_element_type=F32).astype(BF16)
        for q in range(2):
            outer[:, pl.ds(pl.multiple_of((p * 2 + q) * proj, proj), proj), :] = o[:, q * cols : (q + 1) * cols].reshape(
                n_i, proj, cols
            )
        return 0

    lax.fori_loop(0, proj // 2, one_pair, 0)
    w = w_ref[...]
    bias = b_ref[...]

    def one_out(p, _):
        rhs = jnp.concatenate([outer[p * 2], outer[p * 2 + 1]], axis=1)
        res = jnp.dot(w, rhs, preferred_element_type=F32)
        for q in range(2):
            out_ref[p * 2 + q] = (res[:, q * cols : (q + 1) * cols].T + bias).astype(BF16)
        return 0

    lax.fori_loop(0, n_i // 2, one_out, 0)


def pair(get_left, get_right, sizes, operands, w2, bias):
    import functools

    n_seq, deep, resid, proj, jblocks, iblocks = sizes
    S = n_seq * deep
    n_i, n_j, cz = iblocks * resid, jblocks * resid, w2.shape[0]
    return pl.pallas_call(
        functools.partial(pair_kernel, get_left, get_right, sizes),
        out_shape=jax.ShapeDtypeStruct((n_i, n_j, cz), BF16),
        scratch_shapes=[
            pltpu.VMEM((n_i * proj, S), BF16),
            pltpu.VMEM((proj, n_j, S), F32),
            pltpu.VMEM((n_i, proj * proj, n_j), BF16),
        ],
        compiler_params=pltpu.CompilerParams(vmem_limit_bytes=48 * 1024 * 1024),
        name="pair",
    )(*operands, w2, bias.reshape(1, -1))


def spread_weight(w, proj, inv):
    return (w * inv).reshape(proj, proj, -1).transpose(2, 1, 0).reshape(w.shape[1], proj * proj).astype(BF16)
def per_device(x, scale, shift, wl, bl, wr, br, w, b):
    deep, resid, _ = x.shape
    proj = wl.shape[1]
    n_row, n_col, n_seq = (lax.axis_size(a) for a in MESH_AXES)
    left, right = project(x, scale, shift, wl, bl, wr, br, (n_col,), ())
    w2 = spread_weight(w, proj, 1.0 / (deep * n_seq))
    left = lax.all_to_all(left, "col", 0, 0)
    left = lax.all_to_all(left.reshape(n_seq, n_col // n_seq, deep, -1), "seq", 0, 0)
    rows_per = n_row // n_col
    swap = [
        ((r * n_col + c) * n_seq + s, (((r % rows_per) * n_col + c) * n_col + r // rows_per) * n_seq + s)
        for r in range(n_row) for c in range(n_col) for s in range(n_seq)
    ]
    right = lax.ppermute(right, MESH_AXES, swap)
    right = jnp.broadcast_to(right[None], (n_row * n_seq, *right.shape))
    right = lax.all_to_all(right, ("row", "seq"), 0, 0).reshape(n_row, n_seq * deep, -1)
    sizes = (n_seq, deep, resid, proj, n_row, n_col // n_seq)

    def get_left(refs, ib, h):
        return refs[0][:, ib, :, h * 128 : (h + 1) * 128].reshape(n_seq * deep, 128)

    def get_right(refs, jb, h):
        return refs[1][jb, :, h * 128 : (h + 1) * 128]

    return pair(get_left, get_right, sizes, (left, right), w2, b)


def solution(mesh):
    placed = (P("seq", ("row", "col"), None), P(), P(), P(), P(), P(), P(), P(), P())
    return jax.shard_map(
        per_device, mesh=mesh, in_specs=placed, out_specs=P(("row", "seq"), "col", None), check_vma=False
    )
```

```python
import functools

import jax
import jax.numpy as jnp
import numpy as np
from jax import lax
from jax.experimental import pallas as pl
from jax.experimental.pallas import tpu as pltpu
from jax.sharding import PartitionSpec as P

MESH_AXES = ("row", "col", "seq")
Z_HI, Z_LO, CORES = 2, 4, 2
BF16, F32 = jnp.bfloat16, jnp.float32


def project_kernel(*refs):
    n_in = 7
    left_ref, right_ref = refs[n_in : n_in + 2]
    held, sems = refs[n_in + 2 : -1], refs[-1]
    copies = [pltpu.make_async_copy(src, dst, sems.at[i]) for i, (src, dst) in enumerate(zip(refs[:n_in], held))]
    for copy in copies:
        copy.start()
    for copy in copies:
        copy.wait()
    x_ref, scale_ref, shift_ref, wl_ref, bl_ref, wr_ref, br_ref = held
    rows, width = x_ref.shape
    proj = wl_ref.shape[0]
    deep, wide = left_ref.shape[-2:]
    resid = rows // deep
    x = x_ref[...].astype(F32)
    mean = jnp.sum(x, axis=-1, keepdims=True) * (1.0 / width)
    centered = x - mean
    spread = jnp.sum(centered * centered, axis=-1, keepdims=True) * (1.0 / width)
    normed = (centered * lax.rsqrt(spread + 1e-5) * scale_ref[...] + shift_ref[...]).astype(BF16)
    weight = jnp.concatenate([wl_ref[...], wr_ref[...]], axis=0)
    bias = jnp.concatenate([bl_ref[...], br_ref[...]], axis=1)
    both = lax.dot_general(normed, weight, (((1,), (1,)), ((), ())), preferred_element_type=F32)
    both = (both + bias).astype(BF16)
    chan = lax.broadcasted_iota(jnp.int32, (2 * proj, 2 * wide), 0)
    lane = lax.broadcasted_iota(jnp.int32, (2 * proj, 2 * wide), 1)
    wanted = jnp.where(lane < wide, lane % proj, proj + (lane - wide) // resid)
    expand = jnp.where(chan == wanted, 1.0, 0.0).astype(BF16)
    spread_out = jnp.dot(both, expand, preferred_element_type=F32)
    lane = lax.broadcasted_iota(jnp.int32, (resid, 2 * wide), 1)
    own = lax.broadcasted_iota(jnp.int32, (resid, 2 * wide), 0)
    keep = jnp.where(own == jnp.where(lane < wide, lane // proj, lane % resid), 1.0, 0.0)
    kept = (spread_out.reshape(deep, resid, 2 * wide) * keep[None]).reshape(rows, 2 * wide).astype(BF16)
    seq = lax.broadcasted_iota(jnp.int32, (deep, rows), 0)
    tok = lax.broadcasted_iota(jnp.int32, (deep, rows), 1)
    fold = jnp.where(tok // resid == seq, 1.0, 0.0).astype(BF16)
    packed = jnp.dot(fold, kept, preferred_element_type=F32).astype(BF16)
    left_ref[...] = jnp.broadcast_to(packed[:, :wide], left_ref.shape)
    right_ref[...] = jnp.broadcast_to(packed[:, wide:], right_ref.shape)


def project(x, scale, shift, wl, bl, wr, br, left_copies, right_copies):
    deep, resid, width = x.shape
    proj = wl.shape[1]
    operands = (
        x.reshape(deep * resid, width),
        scale.reshape(1, -1),
        shift.reshape(1, -1),
        wl.T,
        bl.reshape(1, -1),
        wr.T,
        br.reshape(1, -1),
    )
    return pl.pallas_call(
        project_kernel,
        in_specs=[pl.BlockSpec(memory_space=pltpu.HBM)] * len(operands),
        scratch_shapes=[*(pltpu.VMEM(a.shape, a.dtype) for a in operands), pltpu.SemaphoreType.DMA((len(operands),))],
        out_shape=[
            jax.ShapeDtypeStruct((*left_copies, deep, resid * proj), BF16),
            jax.ShapeDtypeStruct((*right_copies, deep, resid * proj), BF16),
        ],
        compiler_params=pltpu.CompilerParams(vmem_limit_bytes=60 * 1024 * 1024),
        name="project",
    )(*operands)


def pair_kernel(sizes, *refs):
    n_seq, deep, resid, proj, jblocks, iblocks = sizes
    own_ref, near_ref, far_ref, right_ref, place_ref, w_ref, b_ref, out_ref, lt, rt, outer = refs
    left_refs = [own_ref, near_ref, far_ref.at[0], far_ref.at[1]]
    seqs = [place_ref[i] for i in range(n_seq)]
    depth, lanes = n_seq * deep, 128
    per_r = lanes // resid
    halves = resid * proj // lanes
    n_i, cols = iblocks * resid, jblocks * resid
    for ib in range(iblocks):
        for h in range(halves):
            own = [left_ref[place_ref[n_seq + ib], :, h * lanes : (h + 1) * lanes] for left_ref in left_refs]
            lt[pl.ds((ib * halves + h) * lanes, lanes), :] = jnp.concatenate(own).astype(F32).T.astype(BF16)
    for jb in range(jblocks):
        at = place_ref[n_seq + iblocks + jb]
        for h in range(halves):
            own = jnp.concatenate([right_ref[s, at, :, h * lanes : (h + 1) * lanes] for s in seqs])
            rt[pl.ds(h * per_r, per_r), pl.ds(jb * resid, resid), :] = own.astype(F32).T.reshape(per_r, resid, depth)
    left = lt[...]
    for p in range(proj // 2):
        r = rt[pl.ds(p * 2, 2)].reshape(2 * cols, depth).astype(BF16)
        o = lax.dot_general(left, r, (((1,), (1,)), ((), ())), preferred_element_type=F32).astype(BF16)
        for q in range(2):
            outer[:, pl.ds((p * 2 + q) * proj, proj), :] = o[:, q * cols : (q + 1) * cols].reshape(n_i, proj, cols)
    w = w_ref[...]
    bias = b_ref[...]
    for p in range(n_i // 2):
        rhs = jnp.concatenate([outer[p * 2], outer[p * 2 + 1]], axis=1)
        res = jnp.dot(w, rhs, preferred_element_type=F32)
        for q in range(2):
            out_ref[p * 2 + q] = (res[:, q * cols : (q + 1) * cols].T + bias).astype(BF16)


def pair(sizes, parts, right, place, w2, bias):
    n_seq, deep, resid, proj, jblocks, iblocks = sizes
    n_i, n_j, cz = iblocks * resid, jblocks * resid, w2.shape[0]
    in_vmem = pl.BlockSpec(memory_space=pltpu.VMEM)
    return pl.pallas_call(
        functools.partial(pair_kernel, sizes),
        in_specs=[in_vmem] * (len(parts) + 1) + [pl.BlockSpec(memory_space=pltpu.SMEM), in_vmem, in_vmem],
        out_shape=jax.ShapeDtypeStruct((n_i, n_j, cz), BF16),
        scratch_shapes=[
            pltpu.VMEM((n_i * proj, n_seq * deep), BF16),
            pltpu.VMEM((proj, n_j, n_seq * deep), F32),
            pltpu.VMEM((n_i, proj * proj, n_j), BF16),
        ],
        compiler_params=pltpu.CompilerParams(vmem_limit_bytes=48 * 1024 * 1024),
        name="pair",
    )(*parts, right, place, w2, bias.reshape(1, -1))


def spread_weight(w, proj, inv):
    return (w * inv).reshape(proj, proj, -1).transpose(2, 1, 0).reshape(w.shape[1], proj * proj).astype(BF16)
def ring(a, b, n):
    return min((a - b) % n, (b - a) % n)


def homes(n_row, n_col):
    n_y, per = n_row // Z_HI, n_row // n_col
    near, far = {}, {}
    for goal in range(n_col):
        src = goal * per // n_y
        first = goal * per % n_y
        z_to = [hi * Z_LO + goal // CORES for hi in range(Z_HI)]
        away = {lo: [ring(src * Z_LO + lo, z, Z_HI * Z_LO) for z in z_to] for lo in range(Z_LO)}
        low = sorted(range(Z_LO), key=lambda lo: (away[lo][0], lo))[: Z_LO // Z_HI]
        for pick, maps in ((0, near), (1, far)):
            for hi in range(Z_HI):
                mine = [lo for lo in range(Z_LO) if ((lo in low) == (hi == 0)) == (pick == 0)]
                mine.sort(key=lambda lo: -away[lo][hi])
                for b in range(per):
                    for step, (lo, core) in enumerate((lo, core) for lo in mine for core in range(CORES)):
                        y = (first + b + (step if b else -step)) % n_y
                        maps[src * n_y + first + b, lo * CORES + core] = hi * n_y + y
    return near, far


def left_homes(n_seq):
    out = {}
    for lo in range(Z_LO):
        free = sorted(range(Z_LO), key=lambda z: abs(z - lo))
        for i, s in enumerate(sorted(range(n_seq), key=lambda s: -ring(s, lo, n_seq))):
            out[lo, s] = free[i]
    return out


def per_device(x, scale, shift, wl, bl, wr, br, w, b):
    deep, resid, _ = x.shape
    proj = wl.shape[1]
    n_row, n_col, n_seq = (lax.axis_size(a) for a in MESH_AXES)
    left, right = project(x, scale, shift, wl, bl, wr, br, (1,), ())
    w2 = spread_weight(w, proj, 1.0 / (deep * n_seq))
    wide = resid * proj
    per, n_y = n_row // n_col, n_row // Z_HI
    at = lambda r, c, s: (r * n_col + c) * n_seq + s
    every = [(r, c, s) for r in range(n_row) for c in range(n_col) for s in range(n_seq)]
    move = lambda a, to: lax.ppermute(a, MESH_AXES, [(at(*d), at(*to(*d))) for d in every])
    maps = homes(n_row, n_col)
    near, far = (move(right, lambda r, c, s: (m[r, c], r // per, s)) for m in maps)
    goals = left_homes(n_seq)
    place = np.zeros((n_col, n_seq, Z_HI, n_seq + CORES + n_row), np.int32)
    for c in range(n_col):
        place[c, :, :, n_seq : n_seq + CORES] = [own ^ c % CORES for own in range(CORES)]
        for (lo, s0), z in goals.items():
            place[c, lo, :, z ^ c // CORES] = s0
    for i, m in enumerate(maps):
        for (r, c), to in m.items():
            place[r // per, :, to // n_y, n_seq + CORES + r % per * n_col + c] = to % n_y * 2 + i
    place = jnp.asarray(place)[lax.axis_index("col"), lax.axis_index("seq"), lax.axis_index("row") // n_y]
    left, far = lax.optimization_barrier((left, far))
    core = move(left, lambda r, c, s: (r, c ^ 1, s))
    two = jnp.stack([near, far])
    two, core = lax.optimization_barrier((two, core))
    groups = [list(range(n_y)), list(range(n_y, n_row))]
    right = lax.all_to_all(jnp.broadcast_to(two[None], (n_y, *two.shape)), "row", 0, 0, axis_index_groups=groups)
    right = right.reshape(n_row, deep, wide)
    left = jnp.concatenate([left, core])
    left = move(left, lambda r, c, s: (r, goals[c // CORES, s] * CORES + c % CORES, c // CORES))
    right, left = lax.optimization_barrier((right, left))
    near = move(left, lambda r, c, s: (r, c ^ CORES, s))
    far = move(jnp.stack([left, near]), lambda r, c, s: (r, c ^ 2 * CORES, s))
    parts = [left, near, far]
    right = lax.all_to_all(jnp.broadcast_to(right[None], (n_seq, *right.shape)), "seq", 0, 0)
    sizes = (n_seq, deep, resid, proj, n_row, n_col // n_seq)
    return pair(sizes, parts, right, place, w2, b)


def solution(mesh):
    placed = (P("seq", ("row", "col"), None), P(), P(), P(), P(), P(), P(), P(), P())
    return jax.shard_map(
        per_device, mesh=mesh, in_specs=placed, out_specs=P(("row", "seq"), "col", None), check_vma=False
    )
```

```python
import functools

import jax
import jax.numpy as jnp
import numpy as np
from jax import lax
from jax.experimental import pallas as pl
from jax.experimental.pallas import tpu as pltpu
from jax.sharding import PartitionSpec as P

MESH_AXES = ("row", "col", "seq")
Z_HI, Z_LO, CORES = 2, 4, 2
BF16, F32 = jnp.bfloat16, jnp.float32


def project_kernel(*refs):
    n_in = 7
    both_ref = refs[n_in]
    held, sems = refs[n_in + 1 : -1], refs[-1]
    copies = [pltpu.make_async_copy(src, dst, sems.at[i]) for i, (src, dst) in enumerate(zip(refs[:n_in], held))]
    for copy in copies:
        copy.start()
    x_ref, scale_ref, shift_ref, wl_ref, bl_ref, wr_ref, br_ref = held
    rows, width = x_ref.shape
    proj = wl_ref.shape[0]
    deep, wide = both_ref.shape[-2:]
    resid = rows // deep
    chan = lax.broadcasted_iota(jnp.int32, (2 * proj, 2 * wide), 0)
    lane = lax.broadcasted_iota(jnp.int32, (2 * proj, 2 * wide), 1)
    wanted = jnp.where(lane < wide, lane % proj, proj + (lane - wide) // resid)
    expand = jnp.where(chan == wanted, 1.0, 0.0).astype(BF16)
    lane = lax.broadcasted_iota(jnp.int32, (resid, 2 * wide), 1)
    own = lax.broadcasted_iota(jnp.int32, (resid, 2 * wide), 0)
    keep = jnp.where(own == jnp.where(lane < wide, lane // proj, lane % resid), 1.0, 0.0)
    seq = lax.broadcasted_iota(jnp.int32, (deep, rows), 0)
    tok = lax.broadcasted_iota(jnp.int32, (deep, rows), 1)
    fold = jnp.where(tok // resid == seq, 1.0, 0.0).astype(BF16)
    copies[0].wait()
    x = x_ref[...].astype(F32)
    mean = jnp.sum(x, axis=-1, keepdims=True) * (1.0 / width)
    centered = x - mean
    spread = jnp.sum(centered * centered, axis=-1, keepdims=True) * (1.0 / width)
    scaled = centered * lax.rsqrt(spread + 1e-5)
    for copy in copies[1:]:
        copy.wait()
    normed = (scaled * scale_ref[...] + shift_ref[...]).astype(BF16)
    weight = jnp.concatenate([wl_ref[...], wr_ref[...]], axis=0)
    bias = jnp.concatenate([bl_ref[...], br_ref[...]], axis=1)
    value = lax.dot_general(normed, weight, (((1,), (1,)), ((), ())), preferred_element_type=F32)
    value = (value + bias).astype(BF16)
    spread_out = jnp.dot(value, expand, preferred_element_type=F32)
    kept = (spread_out.reshape(deep, resid, 2 * wide) * keep[None]).reshape(rows, 2 * wide).astype(BF16)
    packed = jnp.dot(fold, kept, preferred_element_type=F32).astype(BF16)
    both_ref[0] = packed[:, :wide]
    both_ref[1] = packed[:, wide:]


def project(x, scale, shift, wl, bl, wr, br):
    deep, resid, width = x.shape
    proj = wl.shape[1]
    operands = (
        x.reshape(deep * resid, width),
        scale.reshape(1, -1),
        shift.reshape(1, -1),
        wl.T,
        bl.reshape(1, -1),
        wr.T,
        br.reshape(1, -1),
    )
    return pl.pallas_call(
        project_kernel,
        in_specs=[pl.BlockSpec(memory_space=pltpu.HBM)] * len(operands),
        scratch_shapes=[*(pltpu.VMEM(a.shape, a.dtype) for a in operands), pltpu.SemaphoreType.DMA((len(operands),))],
        out_shape=jax.ShapeDtypeStruct((2, deep, resid * proj), BF16),
        compiler_params=pltpu.CompilerParams(vmem_limit_bytes=60 * 1024 * 1024),
        name="project",
    )(*operands)


def places():
    col, seq = lax.axis_index("col"), lax.axis_index("seq")
    half = lax.axis_index("row") // (lax.axis_size("row") // Z_HI)
    per = lax.axis_size("row") // lax.axis_size("col")
    z, core = col // CORES, col % CORES
    seqs = []
    for i in (0, 2, 1, 3):
        at = z ^ (core * 2) ^ i ^ seq
        seqs.append(seq ^ 2 ^ (at % 2 * 3) ^ (at // 2))
    blocks = []
    for b in range(per):
        for lo in range(Z_LO):
            for own in range(CORES):
                blocks.append(home(col, lo, b, half) * 2 + (own ^ half))
    return seqs, core, blocks


def pair_kernel(sizes, *refs):
    n_seq, deep, resid, proj, jblocks, iblocks = sizes
    own_ref, core_ref, near_ref, right_ref, w_ref, b_ref, out_ref, lt, rt, outer = refs
    left_refs = [own_ref, core_ref, near_ref.at[0], near_ref.at[1]]
    seqs, core, blocks = places()
    depth, lanes = n_seq * deep, 128
    per_r = lanes // resid
    halves = resid * proj // lanes
    n_i, cols = iblocks * resid, jblocks * resid
    for ib in range(iblocks):
        for h in range(halves):
            own = [ref[ib ^ core ^ i % CORES, :, h * lanes : (h + 1) * lanes] for i, ref in enumerate(left_refs)]
            lt[pl.ds((ib * halves + h) * lanes, lanes), :] = jnp.concatenate(own).astype(F32).T.astype(BF16)
    for jb in range(jblocks):
        at = blocks[jb]
        for h in range(halves):
            own = jnp.concatenate([right_ref[s, at, :, h * lanes : (h + 1) * lanes] for s in seqs])
            rt[pl.ds(h * per_r, per_r), pl.ds(jb * resid, resid), :] = own.astype(F32).T.reshape(per_r, resid, depth)
    left = lt[...]
    for p in range(proj // 2):
        r = rt[pl.ds(p * 2, 2)].reshape(2 * cols, depth).astype(BF16)
        o = lax.dot_general(left, r, (((1,), (1,)), ((), ())), preferred_element_type=F32).astype(BF16)
        for q in range(2):
            outer[:, pl.ds((p * 2 + q) * proj, proj), :] = o[:, q * cols : (q + 1) * cols].reshape(n_i, proj, cols)
    w = w_ref[...]
    bias = b_ref[...]
    for p in range(n_i // 2):
        rhs = jnp.concatenate([outer[p * 2], outer[p * 2 + 1]], axis=1)
        res = jnp.dot(w, rhs, preferred_element_type=F32)
        for q in range(2):
            out_ref[p * 2 + q] = (res[:, q * cols : (q + 1) * cols].T + bias).astype(BF16)


def pair(sizes, parts, right, w2, bias):
    n_seq, deep, resid, proj, jblocks, iblocks = sizes
    n_i, n_j, cz = iblocks * resid, jblocks * resid, w2.shape[0]
    in_vmem = pl.BlockSpec(memory_space=pltpu.VMEM)
    return pl.pallas_call(
        functools.partial(pair_kernel, sizes),
        in_specs=[in_vmem] * (len(parts) + 3),
        out_shape=jax.ShapeDtypeStruct((n_i, n_j, cz), BF16),
        scratch_shapes=[
            pltpu.VMEM((n_i * proj, n_seq * deep), BF16),
            pltpu.VMEM((proj, n_j, n_seq * deep), F32),
            pltpu.VMEM((n_i, proj * proj, n_j), BF16),
        ],
        compiler_params=pltpu.CompilerParams(vmem_limit_bytes=48 * 1024 * 1024),
        name="pair",
    )(*parts, right, w2, bias.reshape(1, -1))


def spread_weight(w, proj, inv):
    return (w * inv).reshape(proj, proj, -1).transpose(2, 1, 0).reshape(w.shape[1], proj * proj).astype(BF16)
def ring(a, b, n):
    return min((a - b) % n, (b - a) % n)


def home(col, lo, b, half):
    src, upper = col // (Z_HI * CORES), col // CORES % 2
    apart = src ^ upper
    order = (1 - apart) * (3 - lo) + apart * ((1 - src) * (1, 3, 2, 0)[lo] + src * (3, 1, 0, 2)[lo])
    step = half * (3 - order) + (1 - half) * order
    n_y = Z_LO * CORES
    return (col * CORES + b + (step if b else n_y - step)) % n_y


def left_home(lo, s):
    at = lo ^ s
    return lo ^ 3 ^ (at % 2 * 2) ^ (at // 2 * 3)


def per_device(x, scale, shift, wl, bl, wr, br, w, b):
    deep, resid, _ = x.shape
    proj = wl.shape[1]
    n_row, n_col, n_seq = (lax.axis_size(a) for a in MESH_AXES)
    own = project(x, scale, shift, wl, bl, wr, br)
    w2 = spread_weight(w, proj, 1.0 / (deep * n_seq))
    wide = resid * proj
    per, n_y = n_row // n_col, n_row // Z_HI
    at = lambda r, c, s: (r * n_col + c) * n_seq + s
    every = [(r, c, s) for r in range(n_row) for c in range(n_col) for s in range(n_seq)]
    move = lambda a, to: lax.ppermute(a, MESH_AXES, [(at(*d), at(*to(*d))) for d in every])
    other = move(own, lambda r, c, s: (r, c ^ 1, s))
    left, right = (jnp.stack([own[i], other[i]]) for i in range(2))
    right = move(right, lambda r, c, s: (c % CORES * n_y + home(r // per, c // CORES, r % per, c % CORES), r // per, s))
    left = move(left, lambda r, c, s: (r, (left_home(c // CORES, s) ^ c % CORES * 2) * CORES + c % CORES, c // CORES))
    groups = [list(range(n_y)), list(range(n_y, n_row))]
    right = lax.all_to_all(jnp.broadcast_to(right[None], (n_y, *right.shape)), "row", 0, 0, axis_index_groups=groups)
    right = right.reshape(n_row, deep, wide)
    right, left = lax.optimization_barrier((right, left))
    core = move(left, lambda r, c, s: (r, c ^ 1, s))
    near = move(jnp.stack([left, core]), lambda r, c, s: (r, c ^ CORES, s))
    parts = [left, core, near]
    right = lax.all_to_all(jnp.broadcast_to(right[None], (n_seq, *right.shape)), "seq", 0, 0)
    sizes = (n_seq, deep, resid, proj, n_row, n_col // n_seq)
    return pair(sizes, parts, right, w2, b)


def solution(mesh):
    placed = (P("seq", ("row", "col"), None), P(), P(), P(), P(), P(), P(), P(), P())
    return jax.shard_map(
        per_device, mesh=mesh, in_specs=placed, out_specs=P(("row", "seq"), "col", None), check_vma=False
    )
```

```python
import functools

import jax
import jax.numpy as jnp
import numpy as np
from jax import lax
from jax.experimental import pallas as pl
from jax.experimental.pallas import tpu as pltpu
from jax.sharding import PartitionSpec as P

MESH_AXES = ("row", "col", "seq")
Z_HI, Z_LO, CORES = 2, 4, 2
SEQ_ORDER = [2, 3, 1, 0]
BF16, F32 = jnp.bfloat16, jnp.float32


def project_kernel(*refs):
    n_in = 7
    both_ref = refs[n_in]
    held, sems = refs[n_in + 1 : -1], refs[-1]
    copies = [pltpu.make_async_copy(src, dst, sems.at[i]) for i, (src, dst) in enumerate(zip(refs[:n_in], held))]
    for copy in copies:
        copy.start()
    x_ref, scale_ref, shift_ref, wl_ref, bl_ref, wr_ref, br_ref = held
    rows, width = x_ref.shape
    proj = wl_ref.shape[0]
    deep, wide = both_ref.shape[-2:]
    resid = rows // deep
    chan = lax.broadcasted_iota(jnp.int32, (2 * proj, 2 * wide), 0)
    lane = lax.broadcasted_iota(jnp.int32, (2 * proj, 2 * wide), 1)
    wanted = jnp.where(lane < wide, lane % proj, proj + (lane - wide) // resid)
    expand = jnp.where(chan == wanted, 1.0, 0.0).astype(BF16)
    lane = lax.broadcasted_iota(jnp.int32, (resid, 2 * wide), 1)
    own = lax.broadcasted_iota(jnp.int32, (resid, 2 * wide), 0)
    keep = jnp.where(own == jnp.where(lane < wide, lane // proj, lane % resid), 1.0, 0.0)
    seq = lax.broadcasted_iota(jnp.int32, (deep, rows), 0)
    tok = lax.broadcasted_iota(jnp.int32, (deep, rows), 1)
    fold = jnp.where(tok // resid == seq, 1.0, 0.0).astype(BF16)
    copies[0].wait()
    x = x_ref[...].astype(F32)
    mean = jnp.sum(x, axis=-1, keepdims=True) * (1.0 / width)
    centered = x - mean
    spread = jnp.sum(centered * centered, axis=-1, keepdims=True) * (1.0 / width)
    scaled = centered * lax.rsqrt(spread + 1e-5)
    for copy in copies[1:]:
        copy.wait()
    normed = (scaled * scale_ref[...] + shift_ref[...]).astype(BF16)
    weight = jnp.concatenate([wl_ref[...], wr_ref[...]], axis=0)
    bias = jnp.concatenate([bl_ref[...], br_ref[...]], axis=1)
    value = lax.dot_general(normed, weight, (((1,), (1,)), ((), ())), preferred_element_type=F32)
    value = (value + bias).astype(BF16)
    spread_out = jnp.dot(value, expand, preferred_element_type=F32)
    kept = (spread_out.reshape(deep, resid, 2 * wide) * keep[None]).reshape(rows, 2 * wide).astype(BF16)
    packed = jnp.dot(fold, kept, preferred_element_type=F32).astype(BF16)
    both_ref[0] = packed[:, :wide]
    both_ref[1] = packed[:, wide:]


def project(x, scale, shift, wl, bl, wr, br):
    deep, resid, width = x.shape
    proj = wl.shape[1]
    operands = (
        x.reshape(deep * resid, width),
        scale.reshape(1, -1),
        shift.reshape(1, -1),
        wl.T,
        bl.reshape(1, -1),
        wr.T,
        br.reshape(1, -1),
    )
    return pl.pallas_call(
        project_kernel,
        in_specs=[pl.BlockSpec(memory_space=pltpu.HBM)] * len(operands),
        scratch_shapes=[*(pltpu.VMEM(a.shape, a.dtype) for a in operands), pltpu.SemaphoreType.DMA((len(operands),))],
        out_shape=jax.ShapeDtypeStruct((2, deep, resid * proj), BF16),
        compiler_params=pltpu.CompilerParams(vmem_limit_bytes=60 * 1024 * 1024),
        name="project",
    )(*operands)


def places():
    col, seq = lax.axis_index("col"), lax.axis_index("seq")
    half = lax.axis_index("row") // (lax.axis_size("row") // Z_HI)
    per, n_y = lax.axis_size("row") // lax.axis_size("col"), lax.axis_size("row") // Z_HI
    z, core = col // CORES, col % CORES
    seqs = []
    for i in (0, 2, 1, 3):
        at = z ^ (core * 2) ^ i ^ seq
        group = seq ^ 2 ^ (at % 2 * 3) ^ (at // 2)
        seqs.append(sum(jnp.where(group == s, i, 0) for i, s in enumerate(SEQ_ORDER)))
    blocks = []
    for b in range(per):
        for lo in range(Z_LO):
            for own in range(CORES):
                blocks.append((n_y - 1 - home(col, lo, b, half)) * 2 + (own ^ half))
    return seqs, core, blocks


def pair_kernel(sizes, *refs):
    n_seq, deep, resid, proj, jblocks, iblocks = sizes
    own_ref, core_ref, near_ref, right_ref, w_ref, b_ref, out_ref, lt, rt, outer = refs
    left_refs = [own_ref, core_ref, near_ref.at[0], near_ref.at[1]]
    seqs, core, blocks = places()
    depth, lanes = n_seq * deep, 128
    per_r = lanes // resid
    halves = resid * proj // lanes
    n_i, cols = iblocks * resid, jblocks * resid
    for ib in range(iblocks):
        for h in range(halves):
            own = [ref[ib ^ core ^ i % CORES, :, h * lanes : (h + 1) * lanes] for i, ref in enumerate(left_refs)]
            lt[pl.ds((ib * halves + h) * lanes, lanes), :] = jnp.concatenate(own).astype(F32).T.astype(BF16)
    for jb in range(jblocks):
        at = blocks[jb]
        for h in range(halves):
            own = jnp.concatenate([right_ref[s, at, :, h * lanes : (h + 1) * lanes] for s in seqs])
            rt[pl.ds(h * per_r, per_r), pl.ds(jb * resid, resid), :] = own.astype(F32).T.reshape(per_r, resid, depth)
    left = lt[...]
    for p in range(proj // 2):
        r = rt[pl.ds(p * 2, 2)].reshape(2 * cols, depth).astype(BF16)
        o = lax.dot_general(left, r, (((1,), (1,)), ((), ())), preferred_element_type=F32).astype(BF16)
        for q in range(2):
            outer[:, pl.ds((p * 2 + q) * proj, proj), :] = o[:, q * cols : (q + 1) * cols].reshape(n_i, proj, cols)
    w = w_ref[...]
    bias = b_ref[...]
    for p in range(n_i // 2):
        rhs = jnp.concatenate([outer[p * 2], outer[p * 2 + 1]], axis=1)
        res = jnp.dot(w, rhs, preferred_element_type=F32)
        for q in range(2):
            out_ref[p * 2 + q] = (res[:, q * cols : (q + 1) * cols].T + bias).astype(BF16)


def pair(sizes, parts, right, w2, bias):
    n_seq, deep, resid, proj, jblocks, iblocks = sizes
    n_i, n_j, cz = iblocks * resid, jblocks * resid, w2.shape[0]
    in_vmem = pl.BlockSpec(memory_space=pltpu.VMEM)
    return pl.pallas_call(
        functools.partial(pair_kernel, sizes),
        in_specs=[in_vmem] * (len(parts) + 3),
        out_shape=jax.ShapeDtypeStruct((n_i, n_j, cz), BF16),
        scratch_shapes=[
            pltpu.VMEM((n_i * proj, n_seq * deep), BF16),
            pltpu.VMEM((proj, n_j, n_seq * deep), F32),
            pltpu.VMEM((n_i, proj * proj, n_j), BF16),
        ],
        compiler_params=pltpu.CompilerParams(vmem_limit_bytes=48 * 1024 * 1024),
        name="pair",
    )(*parts, right, w2, bias.reshape(1, -1))


def spread_weight(w, proj, inv):
    return (w * inv).reshape(proj, proj, -1).transpose(2, 1, 0).reshape(w.shape[1], proj * proj).astype(BF16)
def ring(a, b, n):
    return min((a - b) % n, (b - a) % n)


def home(col, lo, b, half):
    src, upper = col // (Z_HI * CORES), col // CORES % 2
    apart = src ^ upper
    order = (1 - apart) * (3 - lo) + apart * ((1 - src) * (1, 3, 2, 0)[lo] + src * (3, 1, 0, 2)[lo])
    step = half * (3 - order) + (1 - half) * order
    n_y = Z_LO * CORES
    return (col * CORES + b + (step if b else n_y - step)) % n_y


def left_home(lo, s):
    at = lo ^ s
    return lo ^ 3 ^ (at % 2 * 2) ^ (at // 2 * 3)


def per_device(x, scale, shift, wl, bl, wr, br, w, b):
    deep, resid, _ = x.shape
    proj = wl.shape[1]
    n_row, n_col, n_seq = (lax.axis_size(a) for a in MESH_AXES)
    own = project(x, scale, shift, wl, bl, wr, br)
    w2 = spread_weight(w, proj, 1.0 / (deep * n_seq))
    wide = resid * proj
    per, n_y = n_row // n_col, n_row // Z_HI
    at = lambda r, c, s: (r * n_col + c) * n_seq + s
    every = [(r, c, s) for r in range(n_row) for c in range(n_col) for s in range(n_seq)]
    move = lambda a, to: lax.ppermute(a, MESH_AXES, [(at(*d), at(*to(*d))) for d in every])
    other = move(own, lambda r, c, s: (r, c ^ 1, s))
    left, right = (jnp.stack([own[i], other[i]]) for i in range(2))
    right = move(right, lambda r, c, s: (c % CORES * n_y + home(r // per, c // CORES, r % per, c % CORES), r // per, s))
    left = move(left, lambda r, c, s: (r, (left_home(c // CORES, s) ^ c % CORES * 2) * CORES + c % CORES, c // CORES))
    groups = [list(range(n_y))[::-1], list(range(n_y, n_row))[::-1]]
    right = lax.all_to_all(jnp.broadcast_to(right[None], (n_y, *right.shape)), "row", 0, 0, axis_index_groups=groups)
    right = right.reshape(n_row, deep, wide)
    right, left = lax.optimization_barrier((right, left))
    core = move(left, lambda r, c, s: (r, c ^ 1, s))
    near = move(jnp.stack([left, core]), lambda r, c, s: (r, c ^ CORES, s))
    parts = [left, core, near]
    right = lax.all_to_all(jnp.broadcast_to(right[None], (n_seq, *right.shape)), "seq", 0, 0, axis_index_groups=[SEQ_ORDER])
    sizes = (n_seq, deep, resid, proj, n_row, n_col // n_seq)
    return pair(sizes, parts, right, w2, b)


def solution(mesh):
    placed = (P("seq", ("row", "col"), None), P(), P(), P(), P(), P(), P(), P(), P())
    return jax.shard_map(
        per_device, mesh=mesh, in_specs=placed, out_specs=P(("row", "seq"), "col", None), check_vma=False
    )
```

```python
import functools

import jax
import jax.numpy as jnp
import numpy as np
from jax import lax
from jax.experimental import pallas as pl
from jax.experimental.pallas import tpu as pltpu
from jax.sharding import PartitionSpec as P

MESH_AXES = ("row", "col", "seq")
Z_HI, Z_LO, CORES = 2, 4, 2
SEQ_ORDER = [2, 3, 1, 0]
BF16, F32 = jnp.bfloat16, jnp.float32


def project_kernel(*refs):
    n_in = 7
    both_ref = refs[n_in]
    held, sems = refs[n_in + 1 : -1], refs[-1]
    copies = [pltpu.make_async_copy(src, dst, sems.at[i]) for i, (src, dst) in enumerate(zip(refs[:n_in], held))]
    for copy in copies:
        copy.start()
    x_ref, scale_ref, shift_ref, wl_ref, bl_ref, wr_ref, br_ref = held
    rows, width = x_ref.shape
    proj = wl_ref.shape[0]
    deep, wide = both_ref.shape[-2:]
    resid = rows // deep
    chan = lax.broadcasted_iota(jnp.int32, (2 * proj, 2 * wide), 0)
    lane = lax.broadcasted_iota(jnp.int32, (2 * proj, 2 * wide), 1)
    wanted = jnp.where(lane < wide, lane % proj, proj + (lane - wide) // resid)
    expand = jnp.where(chan == wanted, 1.0, 0.0).astype(BF16)
    lane = lax.broadcasted_iota(jnp.int32, (resid, 2 * wide), 1)
    own = lax.broadcasted_iota(jnp.int32, (resid, 2 * wide), 0)
    keep = jnp.where(own == jnp.where(lane < wide, lane // proj, lane % resid), 1.0, 0.0)
    seq = lax.broadcasted_iota(jnp.int32, (deep, rows), 0)
    tok = lax.broadcasted_iota(jnp.int32, (deep, rows), 1)
    fold = jnp.where(tok // resid == seq, 1.0, 0.0).astype(BF16)
    copies[0].wait()
    x = x_ref[...].astype(F32)
    mean = jnp.sum(x, axis=-1, keepdims=True) * (1.0 / width)
    centered = x - mean
    spread = jnp.sum(centered * centered, axis=-1, keepdims=True) * (1.0 / width)
    scaled = centered * lax.rsqrt(spread + 1e-5)
    for copy in copies[1:]:
        copy.wait()
    normed = (scaled * scale_ref[...] + shift_ref[...]).astype(BF16)
    weight = jnp.concatenate([wl_ref[...], wr_ref[...]], axis=0)
    bias = jnp.concatenate([bl_ref[...], br_ref[...]], axis=1)
    value = lax.dot_general(normed, weight, (((1,), (1,)), ((), ())), preferred_element_type=F32)
    value = (value + bias).astype(BF16)
    spread_out = jnp.dot(value, expand, preferred_element_type=F32)
    kept = (spread_out.reshape(deep, resid, 2 * wide) * keep[None]).reshape(rows, 2 * wide).astype(BF16)
    packed = jnp.dot(fold, kept, preferred_element_type=F32).astype(BF16)
    both_ref[0] = packed[:, :wide]
    both_ref[1] = packed[:, wide:]


def project(x, scale, shift, wl, bl, wr, br):
    deep, resid, width = x.shape
    proj = wl.shape[1]
    operands = (
        x.reshape(deep * resid, width),
        scale.reshape(1, -1),
        shift.reshape(1, -1),
        wl.T,
        bl.reshape(1, -1),
        wr.T,
        br.reshape(1, -1),
    )
    return pl.pallas_call(
        project_kernel,
        in_specs=[pl.BlockSpec(memory_space=pltpu.HBM)] * len(operands),
        scratch_shapes=[*(pltpu.VMEM(a.shape, a.dtype) for a in operands), pltpu.SemaphoreType.DMA((len(operands),))],
        out_shape=jax.ShapeDtypeStruct((2, deep, resid * proj), BF16),
        compiler_params=pltpu.CompilerParams(vmem_limit_bytes=60 * 1024 * 1024),
        name="project",
    )(*operands)


def places():
    col, seq = lax.axis_index("col"), lax.axis_index("seq")
    half = lax.axis_index("row") // (lax.axis_size("row") // Z_HI)
    per, n_y = lax.axis_size("row") // lax.axis_size("col"), lax.axis_size("row") // Z_HI
    z, core = col // CORES, col % CORES
    seqs = []
    for i in (0, 2, 1, 3):
        at = z ^ (core * 2) ^ i ^ seq
        group = seq ^ 2 ^ (at % 2 * 3) ^ (at // 2)
        seqs.append(sum(jnp.where(group == s, i, 0) for i, s in enumerate(SEQ_ORDER)))
    blocks = []
    for b in range(per):
        for lo in range(Z_LO):
            for own in range(CORES):
                blocks.append((n_y - 1 - home(col, lo, b, half)) * 2 + (own ^ half))
    return seqs, core, blocks


def turn_kernel(own_ref, core_ref, near_ref, out_ref):
    core, lanes = lax.axis_index("col") % CORES, 128
    halves = own_ref.shape[-1] // lanes
    refs = [own_ref, core_ref, near_ref.at[0], near_ref.at[1]]
    for ib in range(own_ref.shape[0]):
        for h in range(halves):
            own = [ref[ib ^ core ^ i % CORES, :, h * lanes : (h + 1) * lanes] for i, ref in enumerate(refs)]
            out_ref[pl.ds((ib * halves + h) * lanes, lanes), :] = jnp.concatenate(own).astype(F32).T.astype(BF16)


def turn(parts):
    blocks, deep, wide = parts[0].shape
    return pl.pallas_call(
        turn_kernel,
        out_shape=jax.ShapeDtypeStruct((blocks * wide, Z_LO * deep), BF16),
        compiler_params=pltpu.CompilerParams(vmem_limit_bytes=16 * 1024 * 1024),
        cost_estimate=pl.CostEstimate(flops=0, bytes_accessed=2**18, transcendentals=0),
        name="turn",
    )(*parts)


def pair_kernel(sizes, *refs):
    n_seq, deep, resid, proj, jblocks, iblocks = sizes
    lt, right_ref, w_ref, b_ref, out_ref, rt, outer, done, sems = refs
    seqs, _, blocks = places()
    depth, lanes = n_seq * deep, 128
    per_r = lanes // resid
    halves = resid * proj // lanes
    n_i, cols = iblocks * resid, jblocks * resid
    for jb in range(jblocks):
        at = blocks[jb]
        for h in range(halves):
            own = jnp.concatenate([right_ref[s, at, :, h * lanes : (h + 1) * lanes] for s in seqs])
            rt[pl.ds(h * per_r, per_r), pl.ds(jb * resid, resid), :] = own.astype(F32).T.reshape(per_r, resid, depth)
    left = lt[...]
    for p in range(proj // 2):
        r = rt[pl.ds(p * 2, 2)].reshape(2 * cols, depth).astype(BF16)
        o = lax.dot_general(left, r, (((1,), (1,)), ((), ())), preferred_element_type=F32).astype(BF16)
        for q in range(2):
            outer[:, pl.ds((p * 2 + q) * proj, proj), :] = o[:, q * cols : (q + 1) * cols].reshape(n_i, proj, cols)
    w = w_ref[...]
    bias = b_ref[...]
    copies = []
    for p in range(n_i // 2):
        rhs = jnp.concatenate([outer[p * 2], outer[p * 2 + 1]], axis=1)
        res = jnp.dot(w, rhs, preferred_element_type=F32)
        for q in range(2):
            done[p * 2 + q] = (res[:, q * cols : (q + 1) * cols].T + bias).astype(BF16)
        rows = pl.ds(p * 2, 2)
        copies.append(pltpu.make_async_copy(done.at[rows], out_ref.at[rows], sems.at[p]))
        copies[-1].start()
    for copy in copies:
        copy.wait()


def pair(sizes, left, right, w2, bias):
    n_seq, deep, resid, proj, jblocks, iblocks = sizes
    n_i, n_j, cz = iblocks * resid, jblocks * resid, w2.shape[0]
    in_vmem = pl.BlockSpec(memory_space=pltpu.VMEM)
    return pl.pallas_call(
        functools.partial(pair_kernel, sizes),
        in_specs=[in_vmem] * 4,
        out_specs=pl.BlockSpec(memory_space=pl.ANY),
        out_shape=jax.ShapeDtypeStruct((n_i, n_j, cz), BF16),
        scratch_shapes=[
            pltpu.VMEM((proj, n_j, n_seq * deep), F32),
            pltpu.VMEM((n_i, proj * proj, n_j), BF16),
            pltpu.VMEM((n_i, n_j, cz), BF16),
            pltpu.SemaphoreType.DMA((n_i // 2,)),
        ],
        compiler_params=pltpu.CompilerParams(vmem_limit_bytes=48 * 1024 * 1024),
        name="pair",
    )(left, right, w2, bias.reshape(1, -1))


def spread_weight(w, proj, inv):
    return (w * inv).reshape(proj, proj, -1).transpose(2, 1, 0).reshape(w.shape[1], proj * proj).astype(BF16)
def ring(a, b, n):
    return min((a - b) % n, (b - a) % n)


def home(col, lo, b, half):
    src, upper = col // (Z_HI * CORES), col // CORES % 2
    apart = src ^ upper
    order = (1 - apart) * (3 - lo) + apart * ((1 - src) * (1, 3, 2, 0)[lo] + src * (3, 1, 0, 2)[lo])
    step = half * (3 - order) + (1 - half) * order
    n_y = Z_LO * CORES
    return (col * CORES + b + (step if b else n_y - step)) % n_y


def left_home(lo, s):
    at = lo ^ s
    return lo ^ 3 ^ (at % 2 * 2) ^ (at // 2 * 3)


def per_device(x, scale, shift, wl, bl, wr, br, w, b):
    deep, resid, _ = x.shape
    proj = wl.shape[1]
    n_row, n_col, n_seq = (lax.axis_size(a) for a in MESH_AXES)
    own = project(x, scale, shift, wl, bl, wr, br)
    w2 = spread_weight(w, proj, 1.0 / (deep * n_seq))
    wide = resid * proj
    per, n_y = n_row // n_col, n_row // Z_HI
    at = lambda r, c, s: (r * n_col + c) * n_seq + s
    every = [(r, c, s) for r in range(n_row) for c in range(n_col) for s in range(n_seq)]
    move = lambda a, to: lax.ppermute(a, MESH_AXES, [(at(*d), at(*to(*d))) for d in every])
    other = move(own, lambda r, c, s: (r, c ^ 1, s))
    left, right = (jnp.stack([own[i], other[i]]) for i in range(2))
    right = move(right, lambda r, c, s: (c % CORES * n_y + home(r // per, c // CORES, r % per, c % CORES), r // per, s))
    left = move(left, lambda r, c, s: (r, (left_home(c // CORES, s) ^ c % CORES * 2) * CORES + c % CORES, c // CORES))
    groups = [list(range(n_y))[::-1], list(range(n_y, n_row))[::-1]]
    right = lax.all_to_all(jnp.broadcast_to(right[None], (n_y, *right.shape)), "row", 0, 0, axis_index_groups=groups)
    right = right.reshape(n_row, deep, wide)
    right, left = lax.optimization_barrier((right, left))
    core = move(left, lambda r, c, s: (r, c ^ 1, s))
    near = move(jnp.stack([left, core]), lambda r, c, s: (r, c ^ CORES, s))
    parts = [left, core, near]
    right = lax.all_to_all(jnp.broadcast_to(right[None], (n_seq, *right.shape)), "seq", 0, 0, axis_index_groups=[SEQ_ORDER])
    sizes = (n_seq, deep, resid, proj, n_row, n_col // n_seq)
    return pair(sizes, turn(parts), right, w2, b)


def solution(mesh):
    placed = (P("seq", ("row", "col"), None), P(), P(), P(), P(), P(), P(), P(), P())
    return jax.shard_map(
        per_device, mesh=mesh, in_specs=placed, out_specs=P(("row", "seq"), "col", None), check_vma=False
    )
```

```python
import functools

import jax
import jax.numpy as jnp
import numpy as np
from jax import lax
from jax.experimental import pallas as pl
from jax.experimental.pallas import tpu as pltpu
from jax.sharding import PartitionSpec as P

MESH_AXES = ("row", "col", "seq")
Z_HI, Z_LO, CORES = 2, 4, 2
Y_ORDER = [7, 6, 5, 4, 3, 2, 0, 1]
SEQ_ORDER = [2, 3, 1, 0]
BF16, F32 = jnp.bfloat16, jnp.float32


def project_kernel(*refs):
    n_in = 7
    both_ref = refs[n_in]
    held, sems = refs[n_in + 1 : -1], refs[-1]
    copies = [pltpu.make_async_copy(src, dst, sems.at[i]) for i, (src, dst) in enumerate(zip(refs[:n_in], held))]
    for copy in copies:
        copy.start()
    x_ref, scale_ref, shift_ref, wl_ref, bl_ref, wr_ref, br_ref = held
    rows, width = x_ref.shape
    proj = wl_ref.shape[0]
    deep, wide = both_ref.shape[-2:]
    resid = rows // deep
    chan = lax.broadcasted_iota(jnp.int32, (2 * proj, 2 * wide), 0)
    lane = lax.broadcasted_iota(jnp.int32, (2 * proj, 2 * wide), 1)
    wanted = jnp.where(lane < wide, lane % proj, proj + (lane - wide) // resid)
    expand = jnp.where(chan == wanted, 1.0, 0.0).astype(BF16)
    lane = lax.broadcasted_iota(jnp.int32, (resid, 2 * wide), 1)
    own = lax.broadcasted_iota(jnp.int32, (resid, 2 * wide), 0)
    keep = jnp.where(own == jnp.where(lane < wide, lane // proj, lane % resid), 1.0, 0.0)
    seq = lax.broadcasted_iota(jnp.int32, (deep, rows), 0)
    tok = lax.broadcasted_iota(jnp.int32, (deep, rows), 1)
    fold = jnp.where(tok // resid == seq, 1.0, 0.0).astype(BF16)
    copies[0].wait()
    x = x_ref[...].astype(F32)
    mean = jnp.sum(x, axis=-1, keepdims=True) * (1.0 / width)
    centered = x - mean
    spread = jnp.sum(centered * centered, axis=-1, keepdims=True) * (1.0 / width)
    scaled = centered * lax.rsqrt(spread + 1e-5)
    for copy in copies[1:]:
        copy.wait()
    normed = (scaled * scale_ref[...] + shift_ref[...]).astype(BF16)
    weight = jnp.concatenate([wl_ref[...], wr_ref[...]], axis=0)
    bias = jnp.concatenate([bl_ref[...], br_ref[...]], axis=1)
    value = lax.dot_general(normed, weight, (((1,), (1,)), ((), ())), preferred_element_type=F32)
    value = (value + bias).astype(BF16)
    spread_out = jnp.dot(value, expand, preferred_element_type=F32)
    kept = (spread_out.reshape(deep, resid, 2 * wide) * keep[None]).reshape(rows, 2 * wide).astype(BF16)
    packed = jnp.dot(fold, kept, preferred_element_type=F32).astype(BF16)
    both_ref[0] = packed[:, :wide]
    both_ref[1] = packed[:, wide:]


def project(x, scale, shift, wl, bl, wr, br):
    deep, resid, width = x.shape
    proj = wl.shape[1]
    operands = (
        x.reshape(deep * resid, width),
        scale.reshape(1, -1),
        shift.reshape(1, -1),
        wl.T,
        bl.reshape(1, -1),
        wr.T,
        br.reshape(1, -1),
    )
    return pl.pallas_call(
        project_kernel,
        in_specs=[pl.BlockSpec(memory_space=pltpu.HBM)] * len(operands),
        scratch_shapes=[*(pltpu.VMEM(a.shape, a.dtype) for a in operands), pltpu.SemaphoreType.DMA((len(operands),))],
        out_shape=jax.ShapeDtypeStruct((2, deep, resid * proj), BF16),
        compiler_params=pltpu.CompilerParams(vmem_limit_bytes=60 * 1024 * 1024),
        name="project",
    )(*operands)


def places():
    col, seq = lax.axis_index("col"), lax.axis_index("seq")
    half = lax.axis_index("row") // (lax.axis_size("row") // Z_HI)
    per = lax.axis_size("row") // lax.axis_size("col")
    z, core = col // CORES, col % CORES
    seqs = []
    for i in (0, 2, 1, 3):
        at = z ^ (core * 2) ^ i ^ seq
        group = seq ^ 2 ^ (at % 2 * 3) ^ (at // 2)
        seqs.append(sum(jnp.where(group == s, i, 0) for i, s in enumerate(SEQ_ORDER)))
    blocks = []
    for b in range(per):
        for lo in range(Z_LO):
            for own in range(CORES):
                y = home(col, lo, b, half)
                blocks.append(sum(jnp.where(y == a, i, 0) for i, a in enumerate(Y_ORDER)) * 2 + (own ^ half))
    return seqs, core, blocks


def turn_kernel(own_ref, core_ref, near_ref, out_ref):
    core, lanes = lax.axis_index("col") % CORES, 128
    halves = own_ref.shape[-1] // lanes
    refs = [own_ref, core_ref, near_ref.at[0], near_ref.at[1]]
    for ib in range(own_ref.shape[0]):
        for h in range(halves):
            own = [ref[ib ^ core ^ i % CORES, :, h * lanes : (h + 1) * lanes] for i, ref in enumerate(refs)]
            out_ref[pl.ds((ib * halves + h) * lanes, lanes), :] = jnp.concatenate(own).astype(F32).T.astype(BF16)


def turn(parts):
    blocks, deep, wide = parts[0].shape
    return pl.pallas_call(
        turn_kernel,
        out_shape=jax.ShapeDtypeStruct((blocks * wide, Z_LO * deep), BF16),
        compiler_params=pltpu.CompilerParams(vmem_limit_bytes=16 * 1024 * 1024),
        cost_estimate=pl.CostEstimate(flops=0, bytes_accessed=2**18, transcendentals=0),
        name="turn",
    )(*parts)


def pair_kernel(sizes, *refs):
    n_seq, deep, resid, proj, jblocks, iblocks = sizes
    lt, right_ref, w_ref, b_ref, out_ref, rt, outer, done, sems = refs
    seqs, _, blocks = places()
    depth, lanes = n_seq * deep, 128
    per_r = lanes // resid
    halves = resid * proj // lanes
    n_i, cols = iblocks * resid, jblocks * resid
    for jb in range(jblocks):
        at = blocks[jb]
        for h in range(halves):
            own = jnp.concatenate([right_ref[s, at, :, h * lanes : (h + 1) * lanes] for s in seqs])
            rt[pl.ds(h * per_r, per_r), pl.ds(jb * resid, resid), :] = own.astype(F32).T.reshape(per_r, resid, depth)
    left = lt[...]
    for p in range(proj // 2):
        r = rt[pl.ds(p * 2, 2)].reshape(2 * cols, depth).astype(BF16)
        o = lax.dot_general(left, r, (((1,), (1,)), ((), ())), preferred_element_type=F32).astype(BF16)
        for q in range(2):
            outer[:, pl.ds((p * 2 + q) * proj, proj), :] = o[:, q * cols : (q + 1) * cols].reshape(n_i, proj, cols)
    w = w_ref[...]
    bias = b_ref[...]
    copies = []
    for p in range(n_i // 2):
        rhs = jnp.concatenate([outer[p * 2], outer[p * 2 + 1]], axis=1)
        res = jnp.dot(w, rhs, preferred_element_type=F32)
        for q in range(2):
            done[p * 2 + q] = (res[:, q * cols : (q + 1) * cols].T + bias).astype(BF16)
        rows = pl.ds(p * 2, 2)
        copies.append(pltpu.make_async_copy(done.at[rows], out_ref.at[rows], sems.at[p]))
        copies[-1].start()
    for copy in copies:
        copy.wait()


def pair(sizes, left, right, w2, bias):
    n_seq, deep, resid, proj, jblocks, iblocks = sizes
    n_i, n_j, cz = iblocks * resid, jblocks * resid, w2.shape[0]
    in_vmem = pl.BlockSpec(memory_space=pltpu.VMEM)
    return pl.pallas_call(
        functools.partial(pair_kernel, sizes),
        in_specs=[in_vmem] * 4,
        out_specs=pl.BlockSpec(memory_space=pl.ANY),
        out_shape=jax.ShapeDtypeStruct((n_i, n_j, cz), BF16),
        scratch_shapes=[
            pltpu.VMEM((proj, n_j, n_seq * deep), F32),
            pltpu.VMEM((n_i, proj * proj, n_j), BF16),
            pltpu.VMEM((n_i, n_j, cz), BF16),
            pltpu.SemaphoreType.DMA((n_i // 2,)),
        ],
        compiler_params=pltpu.CompilerParams(vmem_limit_bytes=48 * 1024 * 1024),
        name="pair",
    )(left, right, w2, bias.reshape(1, -1))


def spread_weight(w, proj, inv):
    return (w * inv).reshape(proj, proj, -1).transpose(2, 1, 0).reshape(w.shape[1], proj * proj).astype(BF16)
def ring(a, b, n):
    return min((a - b) % n, (b - a) % n)


def home(col, lo, b, half):
    src, upper = col // (Z_HI * CORES), col // CORES % 2
    apart = src ^ upper
    order = (1 - apart) * (3 - lo) + apart * ((1 - src) * (1, 3, 2, 0)[lo] + src * (3, 1, 0, 2)[lo])
    step = half * (3 - order) + (1 - half) * order
    n_y = Z_LO * CORES
    return (col * CORES + b + (step if b else n_y - step)) % n_y


def left_home(lo, s):
    at = lo ^ s
    return lo ^ 3 ^ (at % 2 * 2) ^ (at // 2 * 3)


def per_device(x, scale, shift, wl, bl, wr, br, w, b):
    deep, resid, _ = x.shape
    proj = wl.shape[1]
    n_row, n_col, n_seq = (lax.axis_size(a) for a in MESH_AXES)
    own = project(x, scale, shift, wl, bl, wr, br)
    w2 = spread_weight(w, proj, 1.0 / (deep * n_seq))
    wide = resid * proj
    per, n_y = n_row // n_col, n_row // Z_HI
    at = lambda r, c, s: (r * n_col + c) * n_seq + s
    every = [(r, c, s) for r in range(n_row) for c in range(n_col) for s in range(n_seq)]
    move = lambda a, to: lax.ppermute(a, MESH_AXES, [(at(*d), at(*to(*d))) for d in every])
    other = move(own, lambda r, c, s: (r, c ^ 1, s))
    left, right = (jnp.stack([own[i], other[i]]) for i in range(2))
    right = move(right, lambda r, c, s: (c % CORES * n_y + home(r // per, c // CORES, r % per, c % CORES), r // per, s))
    left = move(left, lambda r, c, s: (r, (left_home(c // CORES, s) ^ c % CORES * 2) * CORES + c % CORES, c // CORES))
    groups = [[half * n_y + y for y in Y_ORDER] for half in range(Z_HI)]
    right = lax.all_to_all(jnp.broadcast_to(right[None], (n_y, *right.shape)), "row", 0, 0, axis_index_groups=groups)
    right = right.reshape(n_row, deep, wide)
    right, left = lax.optimization_barrier((right, left))
    core = move(left, lambda r, c, s: (r, c ^ 1, s))
    near = move(jnp.stack([left, core]), lambda r, c, s: (r, c ^ CORES, s))
    parts = [left, core, near]
    right = lax.all_to_all(jnp.broadcast_to(right[None], (n_seq, *right.shape)), "seq", 0, 0, axis_index_groups=[SEQ_ORDER])
    sizes = (n_seq, deep, resid, proj, n_row, n_col // n_seq)
    return pair(sizes, turn(parts), right, w2, b)


def solution(mesh):
    placed = (P("seq", ("row", "col"), None), P(), P(), P(), P(), P(), P(), P(), P())
    return jax.shard_map(
        per_device, mesh=mesh, in_specs=placed, out_specs=P(("row", "seq"), "col", None), check_vma=False
    )
```
